32 devices in a mesh: dp: 8 (over y, x, core), tensor: 4 (over z).
Axes of the slice: x: 2, y: 2, z: 4, core: 2. Of those that a mesh axis runs over, the one named last changes fastest.
Arguments:
- tokens: bfloat16 [1024, 8192], P('dp', 'tensor'), may hold values from -6 to 6
- cotangent: bfloat16 [1024, 8192], P('dp', 'tensor'), may hold values from -6 to 6
- up_blocks: bfloat16 [3, 64, 128, 256], P(None, 'tensor'), may hold values from -0.21875 to 0.21875
- up_left: bfloat16 [8192, 128], P('tensor'), may hold values from -0.0625 to 0.0625
- up_right: bfloat16 [128, 16384], P(None, 'tensor'), may hold values from -0.375 to 0.375
- down_blocks: bfloat16 [3, 64, 256, 128], P(None, 'tensor'), may hold values from -0.15625 to 0.15625
- down_left: bfloat16 [16384, 128], P('tensor'), may hold values from -0.046875 to 0.046875
- down_right: bfloat16 [128, 8192], P(None, 'tensor'), may hold values from -0.375 to 0.375
Outputs:
- out: bfloat16 [1024, 8192], P('dp', 'tensor')
- tokens_grad: bfloat16 [1024, 8192], P('dp', 'tensor')
- up_blocks_grad: bfloat16 [3, 64, 128, 256], P(None, 'tensor', 'dp')
- up_left_grad: bfloat16 [8192, 128], P('tensor', 'dp')
- up_right_grad: bfloat16 [128, 16384], P('dp', 'tensor')
- down_blocks_grad: bfloat16 [3, 64, 256, 128], P(None, 'tensor', 'dp')
- down_left_grad: bfloat16 [16384, 128], P('tensor', 'dp')
- down_right_grad: bfloat16 [128, 8192], P('dp', 'tensor')
The draws below stay inside these ranges and needn't reach their ends.
All inputs are finite; a program needn't handle non-finite values.
Results may differ from the reference program's by a relative error of at most 0.03.
Values may be sent and summed in bfloat16 or wider, within the bound.
A program may use at most 64 MiB of HBM per device.

```python
import math
import jax
import jax.numpy as jnp
import numpy as np
from jax import lax

D = 8192
FF = 16384
BLOCK = 128
R = 128
TOK_DEV = 128
FACTORS = 3
HB = 256
TOKENS = 1024
N_DP = 8
N_TENSOR = 4


def levels(stream_key, dims, split, low, largest):
    factor_of, own = 1.0, jax.random.fold_in(stream_key, 6)
    for axis_at, shards_of in split:
        heights = jnp.exp(jax.random.uniform(jax.random.fold_in(own, axis_at), (shards_of,), jnp.float32, low / len(split), largest / len(split)))
        factor_of = factor_of * jnp.repeat(heights, dims[axis_at] // shards_of).reshape([-1 if axis == axis_at else 1 for axis in range(len(dims))])
    return factor_of


def normal_values(key, shape, scale, bound, cuts=(), dtype=jnp.bfloat16):
    values = scale * jax.random.normal(key, shape, jnp.float32)
    if cuts:
        values = values * levels(key, shape, cuts, -0.22, 0.18)
    return jnp.clip(values, -bound, bound).astype(dtype)


def setup_inputs(seed: int = 0) -> dict:
    seeds = jax.random.split(jax.random.key(seed), 9)
    return {
        "tokens": normal_values(seeds[0], (TOKENS, D), 1.0, 6.0, ((0, 8), (1, 4))),
        "cotangent": normal_values(seeds[1], (TOKENS, D), 1.0, 6.0, ((0, 8), (1, 4))),
        "up_blocks": normal_values(seeds[2], (FACTORS, D // BLOCK, BLOCK, HB), (2 * FACTORS * BLOCK) ** -0.5, 0.21875, ((1, 4),)),
        "up_left": normal_values(seeds[3], (D, R), D ** -0.5, 0.0625, ((0, 4),)),
        "up_right": normal_values(seeds[4], (R, FF), (2 * R) ** -0.5, 0.375, ((1, 4),)),
        "down_blocks": normal_values(seeds[5], (FACTORS, D // BLOCK, HB, BLOCK), (2 * FACTORS * HB) ** -0.5, 0.15625, ((1, 4),)),
        "down_left": normal_values(seeds[6], (FF, R), FF ** -0.5, 0.046875, ((0, 4),)),
        "down_right": normal_values(seeds[7], (R, D), (2 * R) ** -0.5, 0.375, ((1, 4),)),
    }


def smooth_gate(values):
    return jax.nn.gelu(values, approximate=False)

def widen(array):
    return array.astype(jnp.float32)

def rounded(array):
    return lax.optimization_barrier(array.astype(jnp.bfloat16)).astype(jnp.float32)

def reference(tokens, cotangent, up_blocks, up_left, up_right, down_blocks, down_left, down_right):
    slab_count = N_TENSOR
    per_slab = D // (BLOCK * N_TENSOR)
    partners = [np.arange(slab_count) ^ (0 if factor == 0 else 1 << factor - 1) for factor in range(FACTORS)]
    up_table = widen(up_blocks).reshape(FACTORS, slab_count, per_slab, BLOCK, HB)
    down_table = widen(down_blocks).reshape(FACTORS, slab_count, per_slab, HB, BLOCK)
    grad_scale = 1.0 / math.sqrt(TOKENS)

    def shard_step(carry, inputs):
        shard_tokens, shard_cot = inputs
        row_count = shard_tokens.shape[0]
        token_slabs = widen(shard_tokens).reshape(row_count, slab_count, per_slab, BLOCK)
        cot_slabs = widen(shard_cot).reshape(row_count, slab_count, per_slab, BLOCK)
        low_up = jnp.dot(shard_tokens, up_left, preferred_element_type=jnp.float32).astype(jnp.bfloat16)
        low_cot = jnp.einsum('nd,rd->nr', widen(shard_cot), widen(down_right)).astype(jnp.bfloat16)
        hidden_pre = jnp.dot(low_up, up_right, preferred_element_type=jnp.float32).reshape(row_count, slab_count, per_slab, HB)
        for factor in range(FACTORS):
            hidden_pre = hidden_pre + jnp.einsum('ntbi,tbih->ntbh', token_slabs[:, partners[factor]], up_table[factor])
        hidden_pre = hidden_pre.reshape(row_count, FF)
        active, gelu_back = jax.vjp(smooth_gate, hidden_pre)
        hidden = active.astype(jnp.bfloat16)
        hidden_slabs = widen(hidden).reshape(row_count, slab_count, per_slab, HB)
        low_down = jnp.dot(hidden, down_left, preferred_element_type=jnp.float32).astype(jnp.bfloat16)
        out_sum = jnp.dot(low_down, down_right, preferred_element_type=jnp.float32).reshape(row_count, slab_count, per_slab, BLOCK)
        for factor in range(FACTORS):
            partial_value = jnp.einsum('nsbh,sbhi->nsbi', hidden_slabs, down_table[factor])
            out_sum = out_sum + partial_value[:, partners[factor]]
        shard_out = out_sum.reshape(row_count, D).astype(jnp.bfloat16)
        hidden_grad = jnp.einsum('nr,hr->nh', widen(low_cot), widen(down_left)).reshape(row_count, slab_count, per_slab, HB)
        for factor in range(FACTORS):
            hidden_grad = hidden_grad + jnp.einsum('nsbi,sbhi->nsbh', cot_slabs[:, partners[factor]], down_table[factor])
        pre_grad = gelu_back(hidden_grad.reshape(row_count, FF))[0].astype(jnp.bfloat16)
        pre_slabs = widen(pre_grad).reshape(row_count, slab_count, per_slab, HB)
        low_pre = jnp.einsum('nh,rh->nr', widen(pre_grad), widen(up_right)).astype(jnp.bfloat16)
        token_sum = jnp.einsum('nr,dr->nd', widen(low_pre), widen(up_left)).reshape(row_count, slab_count, per_slab, BLOCK)
        for factor in range(FACTORS):
            partial_value = jnp.einsum('ntbh,tbih->ntbi', pre_slabs, up_table[factor])
            token_sum = token_sum + partial_value[:, partners[factor]]
        shard_grad = token_sum.reshape(row_count, D).astype(jnp.bfloat16)
        up_terms = jnp.stack([jnp.einsum('ntbi,ntbh->tbih', token_slabs[:, partners[factor]], pre_slabs) for factor in range(FACTORS)])
        down_terms = jnp.stack([jnp.einsum('nsbh,nsbi->sbhi', hidden_slabs, cot_slabs[:, partners[factor]]) for factor in range(FACTORS)])
        terms = (up_terms.reshape(FACTORS, slab_count * per_slab, BLOCK, HB), jnp.einsum('nd,nr->dr', widen(shard_tokens), widen(low_pre)), jnp.einsum('nr,nh->rh', widen(low_up), widen(pre_grad)), down_terms.reshape(FACTORS, slab_count * per_slab, HB, BLOCK), jnp.einsum('nh,nr->hr', widen(hidden), widen(low_cot)), jnp.einsum('nr,nd->rd', widen(low_down), widen(shard_cot)))
        carry = tuple((total + rounded(term * grad_scale) for total, term in zip(carry, terms)))
        return (carry, (shard_out, shard_grad))
    start = (jnp.zeros((FACTORS, D // BLOCK, BLOCK, HB), jnp.float32), jnp.zeros((D, R), jnp.float32), jnp.zeros((R, FF), jnp.float32), jnp.zeros((FACTORS, D // BLOCK, HB, BLOCK), jnp.float32), jnp.zeros((FF, R), jnp.float32), jnp.zeros((R, D), jnp.float32))
    stacked = (tokens.reshape(N_DP, TOK_DEV, D), cotangent.reshape(N_DP, TOK_DEV, D))
    sums, results = lax.scan(shard_step, start, stacked)
    out = results[0].reshape(TOKENS, D)
    tokens_grad = results[1].reshape(TOKENS, D)
    grads = tuple((total.astype(jnp.bfloat16) for total in sums))
    return (out, tokens_grad, grads[0], grads[1], grads[2], grads[3], grads[4], grads[5])
```

```python
import functools
import math

import jax
import jax.numpy as jnp
from jax import lax
from jax.experimental import pallas as pl
from jax.experimental.pallas import tpu as pltpu
from jax.sharding import PartitionSpec as P


def partner(block, axis, bit):
    count = lax.axis_size(axis)
    route = []
    for low in range(count):
        high = low | 1 << bit
        if high != low and high < count:
            route += [(low, high), (high, low)]
    return lax.ppermute(block, axis, route)


def smooth_gate(values):
    return jax.nn.gelu(values, approximate=False)


def blockwise(left, blocks, form, width_out):
    row_count = left.shape[0]
    block_count = blocks.shape[0]
    pieces = left.reshape(row_count, block_count, -1)
    result = jnp.einsum(form, pieces, blocks, preferred_element_type=jnp.float32)
    return result.reshape(row_count, block_count * width_out)


def block_outer(left, right, block_count, form):
    row_count = left.shape[0]
    left_pieces = left.reshape(row_count, block_count, -1)
    right_pieces = right.reshape(row_count, block_count, -1)
    return jnp.einsum(form, left_pieces, right_pieces, preferred_element_type=jnp.float32)


def body(tokens, cotangent, up_blocks, up_left, up_right, down_blocks, down_left, down_right):
    row_count = tokens.shape[0]
    block_count = up_blocks.shape[1]
    block_side = up_blocks.shape[2]
    hidden_side = up_blocks.shape[3]
    sections = lax.axis_size("tensor").bit_length() - 1
    section_bits = list(range(sections))
    grad_scale = 1.0 / math.sqrt(row_count * lax.axis_size("dp"))
    low_sums = lax.psum(
        (
            jnp.dot(tokens, up_left, preferred_element_type=jnp.float32),
            jnp.einsum("nd,rd->nr", cotangent, down_right, preferred_element_type=jnp.float32),
        ),
        "tensor",
    )
    low_up = low_sums[0].astype(jnp.bfloat16)
    low_cot = low_sums[1].astype(jnp.bfloat16)
    hidden_pre = blockwise(tokens, up_blocks[0], "nbi,bih->nbh", hidden_side)
    hidden_pre = hidden_pre + jnp.dot(low_up, up_right, preferred_element_type=jnp.float32)
    partner_tokens = {}
    partner_cot = {}
    for section_bit in section_bits:
        arrived = partner((tokens, cotangent), "tensor", section_bit)
        partner_tokens[section_bit] = arrived[0]
        partner_cot[section_bit] = arrived[1]
        hidden_pre = hidden_pre + blockwise(
            arrived[0], up_blocks[section_bit + 1], "nbi,bih->nbh", hidden_side
        )
    active, gelu_back = jax.vjp(smooth_gate, hidden_pre)
    hidden = active.astype(jnp.bfloat16)
    low_down = lax.psum(
        jnp.dot(hidden, down_left, preferred_element_type=jnp.float32), "tensor"
    ).astype(jnp.bfloat16)
    out_sum = blockwise(hidden, down_blocks[0], "nbh,bhi->nbi", block_side)
    out_sum = out_sum + jnp.dot(low_down, down_right, preferred_element_type=jnp.float32)
    for section_bit in section_bits:
        partial_out = blockwise(hidden, down_blocks[section_bit + 1], "nbh,bhi->nbi", block_side)
        out_sum = out_sum + partner(partial_out, "tensor", section_bit)
    out = out_sum.astype(jnp.bfloat16)
    hidden_grad = jnp.einsum("nr,hr->nh", low_cot, down_left, preferred_element_type=jnp.float32)
    hidden_grad = hidden_grad + blockwise(cotangent, down_blocks[0], "nbi,bhi->nbh", hidden_side)
    for section_bit in section_bits:
        hidden_grad = hidden_grad + blockwise(
            partner_cot[section_bit], down_blocks[section_bit + 1], "nbi,bhi->nbh", hidden_side
        )
    down_block_terms = (
        jnp.stack(
            [block_outer(hidden, cotangent, block_count, "nbh,nbi->bhi")]
            + [
                block_outer(hidden, partner_cot[section], block_count, "nbh,nbi->bhi")
                for section in range(sections)
            ]
        )
        * grad_scale
    )
    down_left_terms = (
        jnp.einsum("nh,nr->hr", hidden, low_cot, preferred_element_type=jnp.float32) * grad_scale
    )
    down_right_terms = (
        jnp.einsum("nr,nd->rd", low_down, cotangent, preferred_element_type=jnp.float32)
        * grad_scale
    )
    pre_grad = gelu_back(hidden_grad)[0].astype(jnp.bfloat16)
    low_pre = lax.psum(
        jnp.einsum("nh,rh->nr", pre_grad, up_right, preferred_element_type=jnp.float32), "tensor"
    ).astype(jnp.bfloat16)
    tokens_sum = jnp.einsum("nr,dr->nd", low_pre, up_left, preferred_element_type=jnp.float32)
    tokens_sum = tokens_sum + blockwise(pre_grad, up_blocks[0], "nbh,bih->nbi", block_side)
    for section_bit in section_bits:
        partial_grad = blockwise(pre_grad, up_blocks[section_bit + 1], "nbh,bih->nbi", block_side)
        tokens_sum = tokens_sum + partner(partial_grad, "tensor", section_bit)
    tokens_grad = tokens_sum.astype(jnp.bfloat16)
    up_block_terms = (
        jnp.stack(
            [block_outer(tokens, pre_grad, block_count, "nbi,nbh->bih")]
            + [
                block_outer(partner_tokens[section], pre_grad, block_count, "nbi,nbh->bih")
                for section in range(sections)
            ]
        )
        * grad_scale
    )
    up_left_terms = (
        jnp.einsum("nd,nr->dr", tokens, low_pre, preferred_element_type=jnp.float32) * grad_scale
    )
    up_right_terms = (
        jnp.einsum("nr,nh->rh", low_up, pre_grad, preferred_element_type=jnp.float32) * grad_scale
    )
    summed = (
        lax.psum_scatter(
            up_block_terms.astype(jnp.bfloat16), "dp", scatter_dimension=2, tiled=True
        ).astype(jnp.float32),
        lax.psum_scatter(
            up_left_terms.astype(jnp.bfloat16), "dp", scatter_dimension=1, tiled=True
        ).astype(jnp.float32),
        lax.psum_scatter(
            up_right_terms.astype(jnp.bfloat16), "dp", scatter_dimension=0, tiled=True
        ).astype(jnp.float32),
        lax.psum_scatter(
            down_block_terms.astype(jnp.bfloat16), "dp", scatter_dimension=2, tiled=True
        ).astype(jnp.float32),
        lax.psum_scatter(
            down_left_terms.astype(jnp.bfloat16), "dp", scatter_dimension=1, tiled=True
        ).astype(jnp.float32),
        lax.psum_scatter(
            down_right_terms.astype(jnp.bfloat16), "dp", scatter_dimension=0, tiled=True
        ).astype(jnp.float32),
    )
    grads = tuple((total.astype(jnp.bfloat16) for total in summed))
    return (out, tokens_grad, grads[0], grads[1], grads[2], grads[3], grads[4], grads[5])


MESH = pl.DeviceIdType.MESH
BF = jnp.bfloat16
F32 = jnp.float32


def dot(left, right, left_dim, right_dim):
    return lax.dot_general(
        left, right, (((left_dim,), (right_dim,)), ((), ())), preferred_element_type=F32
    )


def fused_kernel(
    grad_scale,
    tok, cot, up, upl, upr, dn, dnl, dnr,
    out, tgrad, upg, uplg, uprg, dng, dnlg, dnrg,
    ptok, pcot, hp, hg, hid, pre, oacc, tacc, osend, orecv, tsend, trecv,
    lowacc, lowsend, lowrecv, ldacc, ldsend, ldrecv, lpacc, lpsend, lprecv, lows,
    g_d, g_u, g_s, a_d, a_u, a_s, b_d, b_u, b_s, c_d, c_u, c_s,
    send_sem, recv_sem,
):
    blocks = up.shape[1]
    side = up.shape[2]
    wide = up.shape[3]
    rank = upl.shape[1]
    block_cols = 3 * blocks * wide
    me = lax.axis_index("tensor")
    dp = lax.axis_index("dp")
    core = lax.rem(dp, 2)
    x = lax.rem(lax.div(dp, 2), 2)
    y = lax.div(dp, 4)
    peers = [
        me + 1 - 2 * lax.rem(me, 2),
        me + 2 - 4 * lax.div(me, 2),
        3 - me,
    ]
    core_n = dp + 1 - 2 * core
    x_n = dp + 2 - 4 * x
    y_n = dp + 4 - 8 * y
    barrier = pltpu.get_barrier_semaphore()
    for peer in peers:
        pl.semaphore_signal(barrier, inc=1, device_id={"tensor": peer}, device_id_type=MESH)
    for peer in (core_n, x_n, y_n):
        pl.semaphore_signal(barrier, inc=1, device_id={"dp": peer}, device_id_type=MESH)
    pl.semaphore_wait(barrier, 6)

    count = [0]

    def send(src, dst, axis, peer):
        at = count[0]
        count[0] += 1
        copy = pltpu.make_async_remote_copy(
            src_ref=src, dst_ref=dst, send_sem=send_sem.at[at], recv_sem=recv_sem.at[at],
            device_id={axis: peer}, device_id_type=MESH,
        )
        copy.start()
        return copy

    def wait(copies):
        for copy in copies:
            copy.wait()

    def cols(b, width):
        return pl.ds(pl.multiple_of(b * width, width), width)

    def loop(steps, step):
        def run(i, carry):
            step(i)
            return carry
        lax.fori_loop(0, steps, run, 0)

    tok_copies = [send(tok, ptok.at[k], "tensor", peers[k]) for k in (1, 0)]
    lowacc[:, :rank] = dot(tok[...], upl[...], 1, 0)
    lowacc[:, rank:] = dot(cot[...], dnr[...], 1, 1)
    lowsend[...] = lowacc[...].astype(BF)
    low_copies = [send(lowsend, lowrecv.at[k], "tensor", peers[k]) for k in range(3)]
    cot_copies = [send(cot, pcot.at[k], "tensor", peers[k]) for k in (1, 0)]

    def own_factor(b):
        hp[:, cols(b, wide)] = dot(tok[:, cols(b, side)], up[0, b], 1, 0)
        hg[:, cols(b, wide)] = dot(cot[:, cols(b, side)], dn[0, b], 1, 1)

    loop(blocks, own_factor)
    wait(low_copies)
    low_all = lowacc[...]
    for k in range(3):
        low_all = low_all + lowrecv[k].astype(F32)
    lows[0] = low_all[:, :rank].astype(BF)
    lows[1] = low_all[:, rank:].astype(BF)

    def low_factor(b):
        hp[:, cols(b, wide)] += dot(lows[0], upr[:, cols(b, wide)], 1, 0)
        hg[:, cols(b, wide)] += dot(lows[1], dnl[cols(b, wide), :], 1, 1)

    loop(blocks, low_factor)
    ldacc[...] = jnp.zeros_like(ldacc)
    lpacc[...] = jnp.zeros_like(lpacc)
    wait(tok_copies)

    def forward(b):
        h = hp[:, cols(b, wide)]
        h = h + dot(ptok[0, :, cols(b, side)], up[1, b], 1, 0)
        h = h + dot(ptok[1, :, cols(b, side)], up[2, b], 1, 0)
        share = 0.5 + 0.5 * lax.erf(h * math.sqrt(0.5))
        hidden = (h * share).astype(BF)
        hid[:, cols(b, wide)] = hidden
        hp[:, cols(b, wide)] = share + h * (jnp.exp(-0.5 * h * h) * (1.0 / math.sqrt(2 * math.pi)))
        ldacc[...] += dot(hidden, dnl[cols(b, wide), :], 1, 0)
        osend[0, :, cols(b, side)] = dot(hidden, dn[1, b], 1, 0).astype(BF)
        osend[1, :, cols(b, side)] = dot(hidden, dn[2, b], 1, 0).astype(BF)
        oacc[:, cols(b, side)] = dot(hidden, dn[0, b], 1, 0)

    loop(blocks, forward)
    ldsend[...] = ldacc[...].astype(BF)
    ld_copies = [send(ldsend, ldrecv.at[k], "tensor", peers[k]) for k in range(3)]
    out_copies = [send(osend.at[k], orecv.at[k], "tensor", peers[k]) for k in (1, 0)]

    def keep(buffer, at, term, part, parts):
        rows = term.shape[0] // 8
        for p in range(8):
            first = p * rows + part * (rows // parts)
            buffer[p % 2, p // 4, p // 2 % 2, :, at] = (
                term[first : first + rows // parts] * grad_scale
            ).astype(BF)

    wait(cot_copies)

    def down_terms(b):
        hidden = hid[:, cols(b, wide)]
        for k in range(3):
            source = cot[:, cols(b, side)] if k == 0 else pcot[k - 1, :, cols(b, side)]
            term = dot(hidden, source, 0, 0)
            for part in range(2):
                at = pl.ds(pl.multiple_of((k * blocks + b) * wide + part * side, side), side)
                keep(g_d, at, term, part, 2)
        at = pl.ds(pl.multiple_of(block_cols + b * wide, wide), wide)
        keep(g_d, at, dot(lows[1], hidden, 0, 0), 0, 1)

    loop(blocks, down_terms)

    def start_core(group, arrived):
        return [send(group.at[1 - core], arrived, "dp", core_n)]

    def start_chip(group, arrived):
        half = group.shape[4] // 2
        copies = []
        for other in range(2):
            copies.append(
                send(group.at[core, other, 1 - x, :, pl.ds(0, half)], arrived.at[other], "dp", x_n)
            )
            copies.append(
                send(
                    group.at[core, 1 - y, other, :, pl.ds(half, half)],
                    arrived.at[2 + other], "dp", y_n,
                )
            )
        return copies

    def start_last(group, arrived):
        half = group.shape[4] // 2
        return [
            send(group.at[core, 1 - y, x, :, pl.ds(0, half)], arrived.at[0], "dp", y_n),
            send(group.at[core, y, 1 - x, :, pl.ds(half, half)], arrived.at[1], "dp", x_n),
        ]

    def add_core(group, arrived):
        def step(i):
            at = cols(i, 512)
            for yy in range(2):
                for xx in range(2):
                    group[core, yy, xx, :, at] = (
                        group[core, yy, xx, :, at].astype(F32) + arrived[yy, xx, :, at].astype(F32)
                    ).astype(BF)
        loop(group.shape[4] // 512, step)

    def add_chip(group, arrived):
        half = group.shape[4] // 2
        def step(i):
            at = cols(i, 512)
            late = pl.ds(pl.multiple_of(half + i * 512, 512), 512)
            for other in range(2):
                group[core, other, x, :, at] = (
                    group[core, other, x, :, at].astype(F32) + arrived[other, :, at].astype(F32)
                ).astype(BF)
                group[core, y, other, :, late] = (
                    group[core, y, other, :, late].astype(F32)
                    + arrived[2 + other, :, at].astype(F32)
                ).astype(BF)
        loop(half // 512, step)

    def total(group, arrived, part, i):
        half = group.shape[4] // 2
        at = pl.ds(pl.multiple_of(part * half + i * wide, wide), wide)
        return (
            group[core, y, x, :, at].astype(F32) + arrived[part, :, cols(i, wide)].astype(F32)
        ).astype(BF)

    def finish(group, arrived, put_block, put_side):
        per_half = group.shape[4] // 2 // wide
        for part in range(2):
            edge = min(max(3 * blocks - part * per_half, 0), per_half)
            if edge:
                loop(edge, lambda i: put_block(part * per_half + i, total(group, arrived, part, i)))
            if edge < per_half:
                def side_step(i):
                    put_side(
                        part * per_half + edge + i - 3 * blocks,
                        total(group, arrived, part, edge + i),
                    )
                loop(per_half - edge, side_step)

    a_d_copies = start_core(g_d, a_d)

    def backward(b):
        g = hg[:, cols(b, wide)]
        g = g + dot(pcot[0, :, cols(b, side)], dn[1, b], 1, 1)
        g = g + dot(pcot[1, :, cols(b, side)], dn[2, b], 1, 1)
        grad = (g * hp[:, cols(b, wide)]).astype(BF)
        pre[:, cols(b, wide)] = grad
        lpacc[...] += dot(grad, upr[:, cols(b, wide)], 1, 1)
        tsend[0, :, cols(b, side)] = dot(grad, up[1, b], 1, 1).astype(BF)
        tsend[1, :, cols(b, side)] = dot(grad, up[2, b], 1, 1).astype(BF)
        tacc[:, cols(b, side)] = dot(grad, up[0, b], 1, 1)

    loop(blocks, backward)
    lpsend[...] = lpacc[...].astype(BF)
    lp_copies = [send(lpsend, lprecv.at[k], "tensor", peers[k]) for k in range(3)]
    grad_copies = [send(tsend.at[k], trecv.at[k], "tensor", peers[k]) for k in (1, 0)]

    wait(a_d_copies)
    add_core(g_d, a_d)
    b_d_copies = start_chip(g_d, b_d)

    def up_terms(b):
        grad = pre[:, cols(b, wide)]
        for k in range(3):
            source = tok[:, cols(b, side)] if k == 0 else ptok[k - 1, :, cols(b, side)]
            at = pl.ds(pl.multiple_of((k * blocks + b) * wide, wide), wide)
            keep(g_u, at, dot(source, grad, 0, 0), 0, 1)
        at = pl.ds(pl.multiple_of(block_cols + b * wide, wide), wide)
        keep(g_u, at, dot(lows[0], grad, 0, 0), 0, 1)

    loop(blocks, up_terms)
    a_u_copies = start_core(g_u, a_u)
    wait(b_d_copies)
    add_chip(g_d, b_d)
    c_d_copies = start_last(g_d, c_d)
    wait(a_u_copies)
    add_core(g_u, a_u)
    b_u_copies = start_chip(g_u, b_u)

    def whole(acc, arrived):
        value = acc[...]
        for k in range(3):
            value = value + arrived[k].astype(F32)
        return value.astype(BF)

    wait(ld_copies)
    lows[2] = whole(ldacc, ldrecv)
    wait(lp_copies)
    lows[3] = whole(lpacc, lprecv)

    def side_terms(b):
        keep(g_s, cols(b, side), dot(lows[2], cot[:, cols(b, side)], 0, 0), 0, 1)
        at = pl.ds(pl.multiple_of((blocks + b) * side, side), side)
        keep(g_s, at, dot(lows[3], tok[:, cols(b, side)], 0, 0), 0, 1)

    loop(blocks, side_terms)
    a_s_copies = start_core(g_s, a_s)
    wait(out_copies)

    def put_out(b):
        at = cols(b, side)
        out[:, at] = (
            oacc[:, at] + dot(lows[2], dnr[:, at], 1, 0)
            + orecv[0, :, at].astype(F32) + orecv[1, :, at].astype(F32)
        ).astype(BF)

    loop(blocks, put_out)
    wait(a_s_copies)
    add_core(g_s, a_s)
    b_s_copies = start_chip(g_s, b_s)
    wait(c_d_copies)

    def put_down(i, value):
        dng[i, :16, :] = value[:, :side]
        dng[i, 16:, :] = value[:, side:]

    def put_down_left(i, value):
        dnlg[:, cols(i, wide)] = value

    finish(g_d, c_d, put_down, put_down_left)
    wait(b_u_copies)
    add_chip(g_u, b_u)
    c_u_copies = start_last(g_u, c_u)
    wait(b_s_copies)
    add_chip(g_s, b_s)
    c_s_copies = start_last(g_s, c_s)
    wait(grad_copies)

    def put_tokens(b):
        at = cols(b, side)
        rows = pl.ds(pl.multiple_of(b * side, side), side)
        tgrad[:, at] = (
            tacc[:, at] + dot(lows[3], upl[rows, :], 1, 1)
            + trecv[0, :, at].astype(F32) + trecv[1, :, at].astype(F32)
        ).astype(BF)

    loop(blocks, put_tokens)
    wait(c_u_copies)

    def put_up(i, value):
        upg[i] = value

    def put_up_right(i, value):
        uprg[:, cols(i, wide)] = value

    finish(g_u, c_u, put_up, put_up_right)
    wait(c_s_copies)

    def put_sides(i):
        dnrg[:, cols(i, wide)] = total(g_s, c_s, 0, i)
        uplg[:, cols(i, wide)] = total(g_s, c_s, 1, i)

    loop(blocks * side // wide, put_sides)


def fused(tokens, cotangent, up_blocks, up_left, up_right, down_blocks, down_left, down_right):
    rows, width = tokens.shape
    factors, blocks, side, wide = up_blocks.shape
    rank = up_left.shape[1]
    hidden = blocks * wide
    n_dp = lax.axis_size("dp")
    grad_scale = 1.0 / math.sqrt(rows * n_dp)
    share = rank // n_dp
    group_cols = (factors * hidden + hidden, factors * hidden + hidden, 2 * width)
    vmem = pltpu.VMEM
    scratch = [
        vmem((2, rows, width), BF), vmem((2, rows, width), BF),
        vmem((rows, hidden), F32), vmem((rows, hidden), F32),
        vmem((rows, hidden), BF), vmem((rows, hidden), BF),
        vmem((rows, width), F32), vmem((rows, width), F32),
        vmem((2, rows, width), BF), vmem((2, rows, width), BF),
        vmem((2, rows, width), BF), vmem((2, rows, width), BF),
        vmem((rows, 2 * rank), F32), vmem((rows, 2 * rank), BF), vmem((3, rows, 2 * rank), BF),
        vmem((rows, rank), F32), vmem((rows, rank), BF), vmem((3, rows, rank), BF),
        vmem((rows, rank), F32), vmem((rows, rank), BF), vmem((3, rows, rank), BF),
        vmem((4, rows, rank), BF),
    ]
    scratch += [vmem((2, 2, 2, share, c), BF) for c in group_cols]
    scratch += [vmem((2, 2, share, c), BF) for c in group_cols]
    scratch += [vmem((4, share, c // 2), BF) for c in group_cols]
    scratch += [vmem((2, share, c // 2), BF) for c in group_cols]
    scratch += [pltpu.SemaphoreType.DMA((38,)), pltpu.SemaphoreType.DMA((38,))]
    shapes = [
        (rows, width), (rows, width), (factors * blocks, side // n_dp, wide), (share, width),
        (share, hidden), (factors * blocks, wide // n_dp, side), (share, hidden), (share, width),
    ]
    got = pl.pallas_call(
        functools.partial(fused_kernel, grad_scale),
        out_shape=[jax.ShapeDtypeStruct(shape, BF) for shape in shapes],
        in_specs=[pl.BlockSpec(memory_space=pltpu.VMEM)] * 8,
        out_specs=[pl.BlockSpec(memory_space=pltpu.VMEM)] * 8,
        scratch_shapes=scratch,
        compiler_params=pltpu.CompilerParams(
            collective_id=0, has_side_effects=True, vmem_limit_bytes=60 * 1024 * 1024
        ),
    )(tokens, cotangent, up_blocks, up_left, up_right, down_blocks, down_left, down_right)
    return (
        got[0],
        got[1],
        got[2].reshape(factors, blocks, side // n_dp, wide),
        got[3].T,
        got[4],
        got[5].reshape(factors, blocks, wide // n_dp, side),
        got[6].T,
        got[7],
    )


def fits(mesh, tokens, up_blocks, up_left):
    return (
        mesh.shape["dp"] == 8
        and mesh.shape["tensor"] == 4
        and tokens.shape[0] == 8 * 128
        and up_blocks.shape == (3, 64, 128, 256)
        and up_left.shape[1] == 128
    )


def solution(mesh):
    in_specs = (
        P("dp", "tensor"),
        P("dp", "tensor"),
        P(None, "tensor", None, None),
        P("tensor", None),
        P(None, "tensor"),
        P(None, "tensor", None, None),
        P("tensor", None),
        P(None, "tensor"),
    )
    out_specs = (
        P("dp", "tensor"),
        P("dp", "tensor"),
        P(None, "tensor", "dp", None),
        P("tensor", "dp"),
        P("dp", "tensor"),
        P(None, "tensor", "dp", None),
        P("tensor", "dp"),
        P("dp", "tensor"),
    )

    def run(*arrays):
        local = fused if fits(mesh, arrays[0], arrays[2], arrays[3]) else body
        return jax.shard_map(
            local, mesh=mesh, in_specs=in_specs, out_specs=out_specs, check_vma=False
        )(*arrays)

    return run
```

```python
import functools
import math

import jax
import jax.numpy as jnp
from jax import lax
from jax.experimental import pallas as pl
from jax.experimental.pallas import tpu as pltpu
from jax.sharding import PartitionSpec as P


def partner(block, axis, bit):
    count = lax.axis_size(axis)
    route = []
    for low in range(count):
        high = low | 1 << bit
        if high != low and high < count:
            route += [(low, high), (high, low)]
    return lax.ppermute(block, axis, route)


def smooth_gate(values):
    return jax.nn.gelu(values, approximate=False)


def blockwise(left, blocks, form, width_out):
    row_count = left.shape[0]
    block_count = blocks.shape[0]
    pieces = left.reshape(row_count, block_count, -1)
    result = jnp.einsum(form, pieces, blocks, preferred_element_type=jnp.float32)
    return result.reshape(row_count, block_count * width_out)


def block_outer(left, right, block_count, form):
    row_count = left.shape[0]
    left_pieces = left.reshape(row_count, block_count, -1)
    right_pieces = right.reshape(row_count, block_count, -1)
    return jnp.einsum(form, left_pieces, right_pieces, preferred_element_type=jnp.float32)


def body(tokens, cotangent, up_blocks, up_left, up_right, down_blocks, down_left, down_right):
    row_count = tokens.shape[0]
    block_count = up_blocks.shape[1]
    block_side = up_blocks.shape[2]
    hidden_side = up_blocks.shape[3]
    sections = lax.axis_size("tensor").bit_length() - 1
    section_bits = list(range(sections))
    grad_scale = 1.0 / math.sqrt(row_count * lax.axis_size("dp"))
    low_sums = lax.psum(
        (
            jnp.dot(tokens, up_left, preferred_element_type=jnp.float32),
            jnp.einsum("nd,rd->nr", cotangent, down_right, preferred_element_type=jnp.float32),
        ),
        "tensor",
    )
    low_up = low_sums[0].astype(jnp.bfloat16)
    low_cot = low_sums[1].astype(jnp.bfloat16)
    hidden_pre = blockwise(tokens, up_blocks[0], "nbi,bih->nbh", hidden_side)
    hidden_pre = hidden_pre + jnp.dot(low_up, up_right, preferred_element_type=jnp.float32)
    partner_tokens = {}
    partner_cot = {}
    for section_bit in section_bits:
        arrived = partner((tokens, cotangent), "tensor", section_bit)
        partner_tokens[section_bit] = arrived[0]
        partner_cot[section_bit] = arrived[1]
        hidden_pre = hidden_pre + blockwise(
            arrived[0], up_blocks[section_bit + 1], "nbi,bih->nbh", hidden_side
        )
    active, gelu_back = jax.vjp(smooth_gate, hidden_pre)
    hidden = active.astype(jnp.bfloat16)
    low_down = lax.psum(
        jnp.dot(hidden, down_left, preferred_element_type=jnp.float32), "tensor"
    ).astype(jnp.bfloat16)
    out_sum = blockwise(hidden, down_blocks[0], "nbh,bhi->nbi", block_side)
    out_sum = out_sum + jnp.dot(low_down, down_right, preferred_element_type=jnp.float32)
    for section_bit in section_bits:
        partial_out = blockwise(hidden, down_blocks[section_bit + 1], "nbh,bhi->nbi", block_side)
        out_sum = out_sum + partner(partial_out, "tensor", section_bit)
    out = out_sum.astype(jnp.bfloat16)
    hidden_grad = jnp.einsum("nr,hr->nh", low_cot, down_left, preferred_element_type=jnp.float32)
    hidden_grad = hidden_grad + blockwise(cotangent, down_blocks[0], "nbi,bhi->nbh", hidden_side)
    for section_bit in section_bits:
        hidden_grad = hidden_grad + blockwise(
            partner_cot[section_bit], down_blocks[section_bit + 1], "nbi,bhi->nbh", hidden_side
        )
    down_block_terms = (
        jnp.stack(
            [block_outer(hidden, cotangent, block_count, "nbh,nbi->bhi")]
            + [
                block_outer(hidden, partner_cot[section], block_count, "nbh,nbi->bhi")
                for section in range(sections)
            ]
        )
        * grad_scale
    )
    down_left_terms = (
        jnp.einsum("nh,nr->hr", hidden, low_cot, preferred_element_type=jnp.float32) * grad_scale
    )
    down_right_terms = (
        jnp.einsum("nr,nd->rd", low_down, cotangent, preferred_element_type=jnp.float32)
        * grad_scale
    )
    pre_grad = gelu_back(hidden_grad)[0].astype(jnp.bfloat16)
    low_pre = lax.psum(
        jnp.einsum("nh,rh->nr", pre_grad, up_right, preferred_element_type=jnp.float32), "tensor"
    ).astype(jnp.bfloat16)
    tokens_sum = jnp.einsum("nr,dr->nd", low_pre, up_left, preferred_element_type=jnp.float32)
    tokens_sum = tokens_sum + blockwise(pre_grad, up_blocks[0], "nbh,bih->nbi", block_side)
    for section_bit in section_bits:
        partial_grad = blockwise(pre_grad, up_blocks[section_bit + 1], "nbh,bih->nbi", block_side)
        tokens_sum = tokens_sum + partner(partial_grad, "tensor", section_bit)
    tokens_grad = tokens_sum.astype(jnp.bfloat16)
    up_block_terms = (
        jnp.stack(
            [block_outer(tokens, pre_grad, block_count, "nbi,nbh->bih")]
            + [
                block_outer(partner_tokens[section], pre_grad, block_count, "nbi,nbh->bih")
                for section in range(sections)
            ]
        )
        * grad_scale
    )
    up_left_terms = (
        jnp.einsum("nd,nr->dr", tokens, low_pre, preferred_element_type=jnp.float32) * grad_scale
    )
    up_right_terms = (
        jnp.einsum("nr,nh->rh", low_up, pre_grad, preferred_element_type=jnp.float32) * grad_scale
    )
    summed = (
        lax.psum_scatter(
            up_block_terms.astype(jnp.bfloat16), "dp", scatter_dimension=2, tiled=True
        ).astype(jnp.float32),
        lax.psum_scatter(
            up_left_terms.astype(jnp.bfloat16), "dp", scatter_dimension=1, tiled=True
        ).astype(jnp.float32),
        lax.psum_scatter(
            up_right_terms.astype(jnp.bfloat16), "dp", scatter_dimension=0, tiled=True
        ).astype(jnp.float32),
        lax.psum_scatter(
            down_block_terms.astype(jnp.bfloat16), "dp", scatter_dimension=2, tiled=True
        ).astype(jnp.float32),
        lax.psum_scatter(
            down_left_terms.astype(jnp.bfloat16), "dp", scatter_dimension=1, tiled=True
        ).astype(jnp.float32),
        lax.psum_scatter(
            down_right_terms.astype(jnp.bfloat16), "dp", scatter_dimension=0, tiled=True
        ).astype(jnp.float32),
    )
    grads = tuple((total.astype(jnp.bfloat16) for total in summed))
    return (out, tokens_grad, grads[0], grads[1], grads[2], grads[3], grads[4], grads[5])


MESH = pl.DeviceIdType.MESH
BF = jnp.bfloat16
F32 = jnp.float32


def dot(left, right, left_dim, right_dim):
    return lax.dot_general(
        left, right, (((left_dim,), (right_dim,)), ((), ())), preferred_element_type=F32
    )


def fused_kernel(
    grad_scale,
    tok, cot, up_far, upl, upr_far, dn_far, dnl_far, dnr,
    out, tgrad, upg, uplg, uprg, dng, dnlg, dnrg,
    ptok, pcot, hp, hg, hid, pre, oacc, tacc, osend, orecv, tsend, trecv,
    lowacc, lowsend, lowrecv, ldacc, ldsend, ldrecv, lpacc, lpsend, lprecv, lows,
    up, upr, dn, dnl,
    g_d, g_e, g_u, g_s, a_d, a_e, a_u, a_s, b_d, b_e, b_u, b_s, c_d, c_e, c_u, c_s,
    send_sem, recv_sem, load_sem,
):
    blocks = up.shape[1]
    side = up.shape[2]
    wide = up.shape[3]
    rank = upl.shape[1]
    block_cols = 3 * blocks * wide
    me = lax.axis_index("tensor")
    dp = lax.axis_index("dp")
    core = lax.rem(dp, 2)
    x = lax.rem(lax.div(dp, 2), 2)
    y = lax.div(dp, 4)
    peers = [
        me + 1 - 2 * lax.rem(me, 2),
        me + 2 - 4 * lax.div(me, 2),
        3 - me,
    ]
    core_n = dp + 1 - 2 * core
    x_n = dp + 2 - 4 * x
    y_n = dp + 4 - 8 * y
    loads = [
        pltpu.make_async_copy(far, near, load_sem.at[at])
        for at, (far, near) in enumerate(
            ((up_far, up), (dn_far, dn), (upr_far, upr), (dnl_far, dnl))
        )
    ]
    for load in loads:
        load.start()
    barrier = pltpu.get_barrier_semaphore()
    for peer in peers:
        pl.semaphore_signal(barrier, inc=1, device_id={"tensor": peer}, device_id_type=MESH)
    for peer in (core_n, x_n, y_n):
        pl.semaphore_signal(barrier, inc=1, device_id={"dp": peer}, device_id_type=MESH)
    pl.semaphore_wait(barrier, 6)

    count = [0]

    def send(src, dst, axis, peer):
        at = count[0]
        count[0] += 1
        copy = pltpu.make_async_remote_copy(
            src_ref=src, dst_ref=dst, send_sem=send_sem.at[at], recv_sem=recv_sem.at[at],
            device_id={axis: peer}, device_id_type=MESH,
        )
        copy.start()
        return copy

    def wait(copies):
        for copy in copies:
            copy.wait()

    def cols(b, width):
        return pl.ds(pl.multiple_of(b * width, width), width)

    def loop(steps, step):
        def run(i, carry):
            step(i)
            return carry
        lax.fori_loop(0, steps, run, 0)

    tok_copies = [send(tok, ptok.at[k], "tensor", peers[k]) for k in (1, 0)]
    lowacc[:, :rank] = dot(tok[...], upl[...], 1, 0)
    lowacc[:, rank:] = dot(cot[...], dnr[...], 1, 1)
    lowsend[...] = lowacc[...].astype(BF)
    low_copies = [send(lowsend, lowrecv.at[k], "tensor", peers[k]) for k in range(3)]
    cot_copies = [send(cot, pcot.at[k], "tensor", peers[k]) for k in (1, 0)]

    def own_factor(b):
        hp[:, cols(b, wide)] = dot(tok[:, cols(b, side)], up[0, b], 1, 0)
        hg[:, cols(b, wide)] = dot(cot[:, cols(b, side)], dn[0, b], 1, 1)

    wait(loads)
    loop(blocks, own_factor)
    wait(low_copies)
    low_all = lowacc[...]
    for k in range(3):
        low_all = low_all + lowrecv[k].astype(F32)
    lows[0] = low_all[:, :rank].astype(BF)
    lows[1] = low_all[:, rank:].astype(BF)

    def low_factor(b):
        hp[:, cols(b, wide)] += dot(lows[0], upr[:, cols(b, wide)], 1, 0)
        hg[:, cols(b, wide)] += dot(lows[1], dnl[cols(b, wide), :], 1, 1)

    loop(blocks, low_factor)
    ldacc[...] = jnp.zeros_like(ldacc)
    lpacc[...] = jnp.zeros_like(lpacc)
    wait(tok_copies)

    def forward(b):
        h = hp[:, cols(b, wide)]
        h = h + dot(ptok[0, :, cols(b, side)], up[1, b], 1, 0)
        h = h + dot(ptok[1, :, cols(b, side)], up[2, b], 1, 0)
        share = 0.5 + 0.5 * lax.erf(h * math.sqrt(0.5))
        hidden = (h * share).astype(BF)
        hid[:, cols(b, wide)] = hidden
        hp[:, cols(b, wide)] = share + h * (jnp.exp(-0.5 * h * h) * (1.0 / math.sqrt(2 * math.pi)))
        ldacc[...] += dot(hidden, dnl[cols(b, wide), :], 1, 0)
        osend[0, :, cols(b, side)] = dot(hidden, dn[1, b], 1, 0).astype(BF)
        osend[1, :, cols(b, side)] = dot(hidden, dn[2, b], 1, 0).astype(BF)
        oacc[:, cols(b, side)] = dot(hidden, dn[0, b], 1, 0)

    loop(blocks, forward)
    ldsend[...] = ldacc[...].astype(BF)
    ld_copies = [send(ldsend, ldrecv.at[k], "tensor", peers[k]) for k in range(3)]

    def keep(buffer, at, term, part, parts):
        rows = term.shape[0] // 8
        for p in range(8):
            first = p * rows + part * (rows // parts)
            buffer[p % 2, p // 4, p // 2 % 2, :, at] = (
                term[first : first + rows // parts] * grad_scale
            ).astype(BF)

    def keep_down(buffer, b, k, source):
        term = dot(hid[:, cols(b, wide)], source, 0, 0)
        for part in range(2):
            at = pl.ds(pl.multiple_of((k * blocks + b) * wide + part * side, side), side)
            keep(buffer, at, term, part, 2)

    def down_terms(b):
        keep_down(g_d, b, 0, cot[:, cols(b, side)])
        at = pl.ds(pl.multiple_of((blocks + b) * wide, wide), wide)
        keep(g_d, at, dot(lows[1], hid[:, cols(b, wide)], 0, 0), 0, 1)

    def partner_down_terms(b):
        for k in range(2):
            keep_down(g_e, b, k, pcot[k, :, cols(b, side)])

    loop(blocks, down_terms)

    def start_core(group, arrived):
        return [send(group.at[1 - core], arrived, "dp", core_n)]

    def start_chip(group, arrived):
        half = group.shape[4] // 2
        copies = []
        for other in range(2):
            copies.append(
                send(group.at[core, other, 1 - x, :, pl.ds(0, half)], arrived.at[other], "dp", x_n)
            )
            copies.append(
                send(
                    group.at[core, 1 - y, other, :, pl.ds(half, half)],
                    arrived.at[2 + other], "dp", y_n,
                )
            )
        return copies

    def start_last(group, arrived):
        half = group.shape[4] // 2
        return [
            send(group.at[core, 1 - y, x, :, pl.ds(0, half)], arrived.at[0], "dp", y_n),
            send(group.at[core, y, 1 - x, :, pl.ds(half, half)], arrived.at[1], "dp", x_n),
        ]

    def add_core(group, arrived):
        def step(i):
            at = cols(i, 512)
            for yy in range(2):
                for xx in range(2):
                    group[core, yy, xx, :, at] = (
                        group[core, yy, xx, :, at].astype(F32) + arrived[yy, xx, :, at].astype(F32)
                    ).astype(BF)
        loop(group.shape[4] // 512, step)

    def add_chip(group, arrived):
        half = group.shape[4] // 2
        def step(i):
            at = cols(i, 512)
            late = pl.ds(pl.multiple_of(half + i * 512, 512), 512)
            for other in range(2):
                group[core, other, x, :, at] = (
                    group[core, other, x, :, at].astype(F32) + arrived[other, :, at].astype(F32)
                ).astype(BF)
                group[core, y, other, :, late] = (
                    group[core, y, other, :, late].astype(F32)
                    + arrived[2 + other, :, at].astype(F32)
                ).astype(BF)
        loop(half // 512, step)

    def total(group, arrived, part, i):
        half = group.shape[4] // 2
        at = pl.ds(pl.multiple_of(part * half + i * wide, wide), wide)
        return (
            group[core, y, x, :, at].astype(F32) + arrived[part, :, cols(i, wide)].astype(F32)
        ).astype(BF)

    def finish(group, arrived, count, put_block, put_side):
        per_half = group.shape[4] // 2 // wide
        for part in range(2):
            edge = min(max(count - part * per_half, 0), per_half)
            if edge:
                loop(edge, lambda i: put_block(part * per_half + i, total(group, arrived, part, i)))
            if edge < per_half:
                def side_step(i):
                    put_side(
                        part * per_half + edge + i - count,
                        total(group, arrived, part, edge + i),
                    )
                loop(per_half - edge, side_step)

    a_d_copies = start_core(g_d, a_d)
    wait(a_d_copies)
    add_core(g_d, a_d)
    b_d_copies = start_chip(g_d, b_d)
    wait(cot_copies)
    out_copies = [send(osend.at[k], orecv.at[k], "tensor", peers[k]) for k in (1, 0)]
    loop(blocks, partner_down_terms)
    a_e_copies = start_core(g_e, a_e)
    wait(b_d_copies)
    add_chip(g_d, b_d)
    c_d_copies = start_last(g_d, c_d)

    def backward(b):
        g = hg[:, cols(b, wide)]
        g = g + dot(pcot[0, :, cols(b, side)], dn[1, b], 1, 1)
        g = g + dot(pcot[1, :, cols(b, side)], dn[2, b], 1, 1)
        grad = (g * hp[:, cols(b, wide)]).astype(BF)
        pre[:, cols(b, wide)] = grad
        lpacc[...] += dot(grad, upr[:, cols(b, wide)], 1, 1)
        tsend[0, :, cols(b, side)] = dot(grad, up[1, b], 1, 1).astype(BF)
        tsend[1, :, cols(b, side)] = dot(grad, up[2, b], 1, 1).astype(BF)
        tacc[:, cols(b, side)] = dot(grad, up[0, b], 1, 1)

    loop(blocks, backward)
    lpsend[...] = lpacc[...].astype(BF)
    lp_copies = [send(lpsend, lprecv.at[k], "tensor", peers[k]) for k in range(3)]
    grad_copies = [send(tsend.at[k], trecv.at[k], "tensor", peers[k]) for k in (1, 0)]

    wait(a_e_copies)
    add_core(g_e, a_e)
    b_e_copies = start_chip(g_e, b_e)

    def up_terms(b):
        grad = pre[:, cols(b, wide)]
        for k in range(3):
            source = tok[:, cols(b, side)] if k == 0 else ptok[k - 1, :, cols(b, side)]
            at = pl.ds(pl.multiple_of((k * blocks + b) * wide, wide), wide)
            keep(g_u, at, dot(source, grad, 0, 0), 0, 1)
        at = pl.ds(pl.multiple_of(block_cols + b * wide, wide), wide)
        keep(g_u, at, dot(lows[0], grad, 0, 0), 0, 1)

    loop(blocks, up_terms)
    a_u_copies = start_core(g_u, a_u)
    wait(b_e_copies)
    add_chip(g_e, b_e)
    c_e_copies = start_last(g_e, c_e)
    wait(a_u_copies)
    add_core(g_u, a_u)
    b_u_copies = start_chip(g_u, b_u)

    def whole(acc, arrived):
        value = acc[...]
        for k in range(3):
            value = value + arrived[k].astype(F32)
        return value.astype(BF)

    wait(ld_copies)
    lows[2] = whole(ldacc, ldrecv)
    wait(lp_copies)
    lows[3] = whole(lpacc, lprecv)

    def side_terms(b):
        keep(g_s, cols(b, side), dot(lows[2], cot[:, cols(b, side)], 0, 0), 0, 1)
        at = pl.ds(pl.multiple_of((blocks + b) * side, side), side)
        keep(g_s, at, dot(lows[3], tok[:, cols(b, side)], 0, 0), 0, 1)

    loop(blocks, side_terms)
    a_s_copies = start_core(g_s, a_s)
    wait(c_d_copies)

    def put_down(i, value):
        dng[i, :16, :] = value[:, :side]
        dng[i, 16:, :] = value[:, side:]

    def put_partner_down(i, value):
        put_down(blocks + i, value)

    def put_down_left(i, value):
        dnlg[:, cols(i, wide)] = value

    finish(g_d, c_d, blocks, put_down, put_down_left)
    wait(a_s_copies)
    add_core(g_s, a_s)
    b_s_copies = start_chip(g_s, b_s)
    wait(c_e_copies)
    finish(g_e, c_e, 2 * blocks, put_partner_down, put_down_left)
    wait(b_u_copies)
    add_chip(g_u, b_u)
    c_u_copies = start_last(g_u, c_u)
    wait(b_s_copies)
    add_chip(g_s, b_s)
    c_s_copies = start_last(g_s, c_s)
    wait(out_copies)

    def put_out(b):
        at = cols(b, side)
        out[:, at] = (
            oacc[:, at] + dot(lows[2], dnr[:, at], 1, 0)
            + orecv[0, :, at].astype(F32) + orecv[1, :, at].astype(F32)
        ).astype(BF)

    loop(blocks, put_out)
    wait(c_u_copies)

    def put_up(i, value):
        upg[i] = value

    def put_up_right(i, value):
        uprg[:, cols(i, wide)] = value

    finish(g_u, c_u, 3 * blocks, put_up, put_up_right)
    wait(grad_copies)

    def put_tokens(b):
        at = cols(b, side)
        rows = pl.ds(pl.multiple_of(b * side, side), side)
        tgrad[:, at] = (
            tacc[:, at] + dot(lows[3], upl[rows, :], 1, 1)
            + trecv[0, :, at].astype(F32) + trecv[1, :, at].astype(F32)
        ).astype(BF)

    loop(blocks, put_tokens)
    wait(c_s_copies)

    def put_sides(i):
        dnrg[:, cols(i, wide)] = total(g_s, c_s, 0, i)
        uplg[:, cols(i, wide)] = total(g_s, c_s, 1, i)

    loop(blocks * side // wide, put_sides)


def fused(tokens, cotangent, up_blocks, up_left, up_right, down_blocks, down_left, down_right):
    rows, width = tokens.shape
    factors, blocks, side, wide = up_blocks.shape
    rank = up_left.shape[1]
    hidden = blocks * wide
    n_dp = lax.axis_size("dp")
    grad_scale = 1.0 / math.sqrt(rows * n_dp)
    share = rank // n_dp
    group_cols = (2 * hidden, (factors - 1) * hidden, (factors + 1) * hidden, 2 * width)
    vmem = pltpu.VMEM
    scratch = [
        vmem((2, rows, width), BF), vmem((2, rows, width), BF),
        vmem((rows, hidden), F32), vmem((rows, hidden), F32),
        vmem((rows, hidden), BF), vmem((rows, hidden), BF),
        vmem((rows, width), F32), vmem((rows, width), F32),
        vmem((2, rows, width), BF), vmem((2, rows, width), BF),
        vmem((2, rows, width), BF), vmem((2, rows, width), BF),
        vmem((rows, 2 * rank), F32), vmem((rows, 2 * rank), BF), vmem((3, rows, 2 * rank), BF),
        vmem((rows, rank), F32), vmem((rows, rank), BF), vmem((3, rows, rank), BF),
        vmem((rows, rank), F32), vmem((rows, rank), BF), vmem((3, rows, rank), BF),
        vmem((4, rows, rank), BF),
        vmem(up_blocks.shape, BF), vmem(up_right.shape, BF),
        vmem(down_blocks.shape, BF), vmem(down_left.shape, BF),
    ]
    scratch += [vmem((2, 2, 2, share, c), BF) for c in group_cols]
    scratch += [vmem((2, 2, share, c), BF) for c in group_cols]
    scratch += [vmem((4, share, c // 2), BF) for c in group_cols]
    scratch += [vmem((2, share, c // 2), BF) for c in group_cols]
    scratch += [pltpu.SemaphoreType.DMA((count,)) for count in (45, 45, 4)]
    shapes = [
        (rows, width), (rows, width), (factors * blocks, side // n_dp, wide), (share, width),
        (share, hidden), (factors * blocks, wide // n_dp, side), (share, hidden), (share, width),
    ]
    got = pl.pallas_call(
        functools.partial(fused_kernel, grad_scale),
        out_shape=[jax.ShapeDtypeStruct(shape, BF) for shape in shapes],
        in_specs=[
            pl.BlockSpec(memory_space=pl.ANY if at in (2, 4, 5, 6) else pltpu.VMEM)
            for at in range(8)
        ],
        out_specs=[pl.BlockSpec(memory_space=pltpu.VMEM)] * 8,
        scratch_shapes=scratch,
        compiler_params=pltpu.CompilerParams(
            collective_id=0, has_side_effects=True, vmem_limit_bytes=60 * 1024 * 1024
        ),
    )(tokens, cotangent, up_blocks, up_left, up_right, down_blocks, down_left, down_right)
    return (
        got[0],
        got[1],
        got[2].reshape(factors, blocks, side // n_dp, wide),
        got[3].T,
        got[4],
        got[5].reshape(factors, blocks, wide // n_dp, side),
        got[6].T,
        got[7],
    )


def fits(mesh, tokens, up_blocks, up_left):
    return (
        mesh.shape["dp"] == 8
        and mesh.shape["tensor"] == 4
        and tokens.shape[0] == 8 * 128
        and up_blocks.shape == (3, 64, 128, 256)
        and up_left.shape[1] == 128
    )


def solution(mesh):
    in_specs = (
        P("dp", "tensor"),
        P("dp", "tensor"),
        P(None, "tensor", None, None),
        P("tensor", None),
        P(None, "tensor"),
        P(None, "tensor", None, None),
        P("tensor", None),
        P(None, "tensor"),
    )
    out_specs = (
        P("dp", "tensor"),
        P("dp", "tensor"),
        P(None, "tensor", "dp", None),
        P("tensor", "dp"),
        P("dp", "tensor"),
        P(None, "tensor", "dp", None),
        P("tensor", "dp"),
        P("dp", "tensor"),
    )

    def run(*arrays):
        local = fused if fits(mesh, arrays[0], arrays[2], arrays[3]) else body
        return jax.shard_map(
            local, mesh=mesh, in_specs=in_specs, out_specs=out_specs, check_vma=False
        )(*arrays)

    return run
```
